512 devices in a mesh: row: 16 (over z_hi, x), col: 32 (over z_lo, y, core).
Axes of the slice: x: 4, y: 4, z: 16 (z_hi: 4, z_lo: 4; z = z_hi * 4 + z_lo), core: 2. Of those that a mesh axis runs over, the one named last changes fastest.
Arguments:
- images: bfloat16 [11264, 1152], P(('row', 'col')), may hold values from -0.1875 to 0.1875
- texts: bfloat16 [11264, 1152], P(('col', 'row')), may hold values from -0.1875 to 0.1875
- logarithmic_scale: float32 [], replicated, may hold values from 2 to 3
- similarity_bias: float32 [], replicated, may hold values from -4 to -1
Outputs:
- grad_images: float32 [11264, 1152], P(('row', 'col'))
- grad_texts: float32 [11264, 1152], P(('col', 'row'))
The draws below stay inside these ranges and needn't reach their ends.
All inputs are finite; a program needn't handle non-finite values.
Results may differ from the reference program's by a relative error of at most 0.03.
Values may be sent and summed in bfloat16 or wider, within the bound.
No kernel may reach another device: no remote copies, remote signals or barrier semaphores. Data moves between devices by JAX's collectives and lax.ppermute only.
A program may use at most 64 MiB of HBM per device.

```python
import jax
import jax.numpy as jnp
from jax import lax

D = 1152
BATCH = 11264
ROW_BLOCK = 704
COL_BLOCK = 352
N_ROW = 16
N_COL = 32


def level_of(own_key, extent, cuts, low, top_value):
    factor_of = 1.0
    for axis_at, shards_of in cuts:
        steps = jax.random.uniform(jax.random.fold_in(jax.random.fold_in(own_key, 6), axis_at), (shards_of,), jnp.float32, low / len(cuts), top_value / len(cuts))
        factor_of = factor_of * jnp.repeat(jnp.exp(steps), extent[axis_at] // shards_of).reshape((-1,) + (1,) * (len(extent) - 1 - axis_at))
    return factor_of


def normal_values(stream_key, shape, width, limit, split=(), kind=jnp.bfloat16):
    factor_of = level_of(stream_key, shape, split, -0.22, 0.18) if split else 1.0
    array = jax.random.normal(stream_key, shape, jnp.float32) * width * factor_of
    return jnp.minimum(jnp.maximum(array, -limit), limit).astype(kind)


def setup_inputs(seed: int = 0) -> dict:
    splits = jax.random.split(jax.random.key(seed), 5)
    images = normal_values(splits[0], (BATCH, D), D ** -0.5, 0.1875, ((0, 512),))
    texts = normal_values(splits[1], (BATCH, D), D ** -0.5, 0.1875, ((0, 512),))
    logarithmic_scale = jnp.clip(jax.random.uniform(splits[2], (), jnp.float32, 2.0, 3.0), 2.0, 3.0)
    similarity_bias = jnp.clip(jax.random.uniform(splits[3], (), jnp.float32, -4.0, -1.0), -4.0, -1.0)
    return dict(images=images, texts=texts, logarithmic_scale=logarithmic_scale, similarity_bias=similarity_bias)


def normalize(values):
    wide = values.astype(jnp.float32)
    length = jnp.sqrt(lax.optimization_barrier(jnp.sum(wide * wide, axis=1, keepdims=True)) + 1e-06)
    return (wide / length, length)

def norm_back(normed, length, upstream):
    along = lax.optimization_barrier(jnp.sum(normed * upstream, axis=1, keepdims=True))
    return (upstream - normed * along) / length

def pairwise_factors(selected_entries, row_offset, column_ranges, column_offset, logit_multiplier, similarity_bias):
    similarity_logits = lax.dot_general(selected_entries, column_ranges, (((1,), (1,)), ((), ())), preferred_element_type=jnp.float32)
    row_ids = row_offset + lax.broadcasted_iota(jnp.int32, similarity_logits.shape, 0)
    col_ids = column_offset + lax.broadcasted_iota(jnp.int32, similarity_logits.shape, 1)
    pair_targets = jnp.where(row_ids == col_ids, jnp.float32(1.0), jnp.float32(-1.0))
    signed_logit = pair_targets * (logit_multiplier * similarity_logits + similarity_bias)
    return (-pair_targets * jax.nn.sigmoid(-signed_logit)).astype(jnp.bfloat16)

def reference(images, texts, logarithmic_scale, similarity_bias):
    img_unit, img_len = normalize(images)
    txt_unit, txt_len = normalize(texts)
    img_bf = img_unit.astype(jnp.bfloat16)
    caption_halfprecision = txt_unit.astype(jnp.bfloat16)
    logit_multiplier = jnp.exp(logarithmic_scale)

    def one_block(carry, block_index):
        begin_offset = (block_index * ROW_BLOCK).astype(jnp.int32)
        selected_entries = lax.dynamic_slice_in_dim(img_bf, begin_offset, ROW_BLOCK, 0)
        sigmoid_factors = pairwise_factors(selected_entries, begin_offset, caption_halfprecision, jnp.int32(0), logit_multiplier, similarity_bias)
        partial_results = jnp.einsum('rgc,gcd->grd', sigmoid_factors.reshape(ROW_BLOCK, N_COL, COL_BLOCK).astype(jnp.float32), caption_halfprecision.reshape(N_COL, COL_BLOCK, D).astype(jnp.float32))
        img_rows = lax.optimization_barrier(jnp.sum(logit_multiplier * partial_results, axis=0))
        caption_portion = logit_multiplier * lax.dot_general(sigmoid_factors, selected_entries, (((0,), (0,)), ((), ())), preferred_element_type=jnp.float32)
        caption_portion = lax.optimization_barrier(caption_portion.astype(jnp.bfloat16))
        return (carry + caption_portion.astype(jnp.float32), img_rows)
    start_carry = jnp.zeros((BATCH, D), jnp.float32)
    grad_txt_unit, img_blocks = lax.scan(one_block, start_carry, jnp.arange(N_ROW, dtype=jnp.int32))
    grad_img_unit = img_blocks.reshape(BATCH, D)
    return (norm_back(img_unit, img_len, grad_img_unit), norm_back(txt_unit, txt_len, grad_txt_unit))
```

```python
import functools

import jax
import jax.numpy as jnp
from jax import lax
from jax.experimental import pallas as pl
from jax.experimental.pallas import tpu as pltpu
from jax.sharding import Mesh
from jax.sharding import PartitionSpec as P

D = 1152
ROWS = 22
PAD = 24
AXES = ("zh", "x", "zl", "y", "core")
SIZES = (4, 4, 4, 4, 2)
IMG_STAGES = (("zl", "pair2"), ("y", "pair3"), ("core", "pair"))
TXT_STAGES = (("zh", "pair3"), ("x", "pair3"))
IMG_BACK = None
TXT_BACK = None
VMEM = 48 * 1024 * 1024


def swap(value, axis, mask):
    size = SIZES[AXES.index(axis)]
    return lax.ppermute(value, axis, [(i, i ^ mask) for i in range(size)])


def order(way):
    return {"pair": (0, 1), "pair2": (0, 1, 2, 3), "pair3": (0, 1, 3, 2), "direct": (0, 1, 3, 2), "a2a": None}[way]


def spread(held, axis, way):
    if way == "pair":
        return jnp.concatenate([held, swap(held, axis, 1)])
    if way in ("pair2", "pair3"):
        held = jnp.concatenate([held, swap(held, axis, 1)])
        return jnp.concatenate([held, swap(held, axis, 2 if way == "pair2" else 3)])
    if way == "direct":
        return jnp.concatenate([held] + [swap(held, axis, m) for m in (1, 3, 2)])
    size = SIZES[AXES.index(axis)]
    out = lax.all_to_all(jnp.broadcast_to(held[None], (size,) + held.shape), axis, 0, 0, tiled=True)
    return out.reshape((-1, held.shape[1]))


def add(parts):
    return sum(p.astype(jnp.float32) for p in parts).astype(jnp.bfloat16)


def collect(held, axis, way):
    size = SIZES[AXES.index(axis)]
    if way in ("pair", "pair2", "pair3"):
        for mask in {"pair": (1,), "pair2": (2, 1), "pair3": (3, 1)}[way]:
            half = held.shape[0] // 2
            held = add([held[:half], swap(held[half:], axis, mask)])
        return held
    parts = held.reshape((size, -1, held.shape[1]))
    if way == "direct":
        return add([parts[0]] + [swap(parts[k], axis, m) for k, m in ((1, 1), (2, 3), (3, 2))])
    parts = lax.all_to_all(parts, axis, 0, 0, tiled=True)
    return add([parts[k] for k in range(size)])


def slots(stages, names):
    coords = {n: lax.axis_index(n) for n in names}
    found = [jnp.int32(0)]
    weight = {}
    total = 1
    for n in reversed(names):
        weight[n] = total
        total *= SIZES[AXES.index(n)]
    for axis, way in stages:
        seq = order(way)
        size = SIZES[AXES.index(axis)]
        here = [jnp.int32(k) if seq is None else coords[axis] ^ seq[k] for k in range(size)]
        found = [f + weight[axis] * h for h in here for f in found]
    return jnp.stack(found)


def unit_kernel(img_ref, txt_ref, img_out, txt_out):
    for src, dst in ((img_ref, img_out), (txt_ref, txt_out)):
        wide = src[...].astype(jnp.float32)
        length = jnp.sqrt(jnp.sum(wide * wide, axis=1, keepdims=True) + 1e-06)
        unit = wide / length
        dst[...] = jnp.concatenate([unit, jnp.zeros((PAD - ROWS, D), jnp.float32)]).astype(jnp.bfloat16)


def pair_kernel(scal_ref, img_ref, txt_ref, row_ref, col_ref, gimg_ref, gtxt_ref, w_ref):
    scale, bias = scal_ref[0], scal_ref[1]
    n = img_ref.shape[0]
    tile = 256
    for t in range(n // tile):
        rows = pl.ds(t * tile, tile)
        s = lax.dot_general(img_ref[rows, :], txt_ref[...], (((1,), (1,)), ((), ())), preferred_element_type=jnp.float32)
        z = scale * s + bias
        same = row_ref[rows, :] == col_ref[...]
        w = jnp.where(same, -1.0, 1.0) / (1.0 + jnp.exp(jnp.where(same, z, -z)))
        w_ref[rows, :] = w.astype(jnp.bfloat16)
    w_all = w_ref[...]
    for t in range(3):
        cols = pl.ds(t * 384, 384)
        g = lax.dot_general(w_all, img_ref[:, cols], (((0,), (0,)), ((), ())), preferred_element_type=jnp.float32)
        gtxt_ref[:, cols] = (scale * g).astype(jnp.bfloat16)
    for t in range(3):
        cols = pl.ds(t * 384, 384)
        g = jnp.dot(w_all, txt_ref[:, cols], preferred_element_type=jnp.float32)
        gimg_ref[:, cols] = (scale * g).astype(jnp.bfloat16)


def back_kernel(img_ref, txt_ref, gi_ref, gt_ref, img_out, txt_out):
    for src, g_ref, dst in ((img_ref, gi_ref, img_out), (txt_ref, gt_ref, txt_out)):
        wide = src[...].astype(jnp.float32)
        length = jnp.sqrt(jnp.sum(wide * wide, axis=1, keepdims=True) + 1e-06)
        unit = wide / length
        g = g_ref[...].astype(jnp.float32)[:ROWS]
        along = jnp.sum(unit * g, axis=1, keepdims=True)
        dst[...] = (g - unit * along) / length


def vm():
    return pl.BlockSpec(memory_space=pltpu.VMEM)


PARAMS = pltpu.CompilerParams(vmem_limit_bytes=VMEM)


def on_device(images, texts, logarithmic_scale, similarity_bias):
    block = jax.ShapeDtypeStruct((PAD, D), jnp.bfloat16)
    img, txt = pl.pallas_call(unit_kernel, out_shape=(block, block), in_specs=[vm()] * 2, out_specs=(vm(), vm()), compiler_params=PARAMS, name="unit")(images, texts)
    for axis, way in TXT_STAGES:
        txt = spread(txt, axis, way)
    for axis, way in IMG_STAGES:
        img = spread(img, axis, way)
    row = lax.axis_index("zh") * 4 + lax.axis_index("x")
    col = (lax.axis_index("zl") * 4 + lax.axis_index("y")) * 2 + lax.axis_index("core")
    img_ids = row * 32 + slots(IMG_STAGES, ("zl", "y", "core"))
    txt_ids = col * 16 + slots(TXT_STAGES, ("zh", "x"))
    within = jnp.arange(PAD, dtype=jnp.int32)
    row_ids = jnp.where(within < ROWS, img_ids[:, None] * ROWS + within, -1).reshape(-1, 1)
    col_ids = jnp.where(within < ROWS, txt_ids[:, None] * ROWS + within, -2).reshape(1, -1)
    scal = jnp.stack([jnp.exp(logarithmic_scale), similarity_bias])
    ni, nt = img.shape[0], txt.shape[0]
    gimg, gtxt = pl.pallas_call(
        pair_kernel,
        out_shape=(jax.ShapeDtypeStruct((ni, D), jnp.bfloat16), jax.ShapeDtypeStruct((nt, D), jnp.bfloat16)),
        in_specs=[pl.BlockSpec(memory_space=pltpu.SMEM)] + [vm()] * 4,
        out_specs=(vm(), vm()),
        scratch_shapes=[pltpu.VMEM((ni, nt), jnp.bfloat16)],
        compiler_params=PARAMS,
        name="pairs",
    )(scal, img, txt, row_ids, col_ids)
    for axis, way in reversed(TXT_BACK or TXT_STAGES):
        gtxt = collect(gtxt, axis, way)
    for axis, way in reversed(IMG_BACK or IMG_STAGES):
        gimg = collect(gimg, axis, way)
    wide = jax.ShapeDtypeStruct((ROWS, D), jnp.float32)
    return pl.pallas_call(back_kernel, out_shape=(wide, wide), in_specs=[vm()] * 4, out_specs=(vm(), vm()), compiler_params=PARAMS, name="back")(images, texts, gimg, gtxt)


def solution(mesh):
    fine = Mesh(mesh.devices.reshape(SIZES), AXES)
    return jax.shard_map(
        on_device,
        mesh=fine,
        in_specs=(P(AXES, None), P(("zl", "y", "core", "zh", "x"), None), P(), P()),
        out_specs=(P(AXES, None), P(("zl", "y", "core", "zh", "x"), None)),
        check_vma=False,
    )
```

```python
import functools

import jax
import jax.numpy as jnp
from jax import lax
from jax.experimental import pallas as pl
from jax.experimental.pallas import tpu as pltpu
from jax.sharding import Mesh
from jax.sharding import PartitionSpec as P

D = 1152
ROWS = 22
PAD = 24
AXES = ("zh", "x", "zl", "y", "core")
SIZES = (4, 4, 4, 4, 2)
OUT = (
    ("t", "zh", (1, 3)),
    ("i", "zl", "a"),
    ("t", "zh", (3, 1)),
    ("i", "y", "a"),
    ("t", "x", (1, 3)),
    ("t", "x", (3, 1)),
    ("i", "core", (1, 1)),
)
BACK = tuple(reversed(OUT))
VMEM = 48 * 1024 * 1024


def swap(value, axis, masks):
    size = SIZES[AXES.index(axis)]
    if axis == "core" or masks[0] == masks[1]:
        return lax.ppermute(value, axis, [(i, i ^ masks[0]) for i in range(size)])
    return lax.ppermute(value, (axis, "core"), [(2 * i + c, 2 * (i ^ masks[c]) + c) for i in range(size) for c in range(2)])


def spread(held, axis, way):
    if way == "a":
        size = SIZES[AXES.index(axis)]
        out = lax.all_to_all(jnp.broadcast_to(held[None], (size,) + held.shape), axis, 0, 0, tiled=True)
        return out.reshape((-1, held.shape[1]))
    return jnp.concatenate([held, swap(held, axis, way)])


def add(parts):
    return sum(p.astype(jnp.float32) for p in parts).astype(jnp.bfloat16)


def collect(held, axis, way):
    if way == "a":
        size = SIZES[AXES.index(axis)]
        parts = lax.all_to_all(held.reshape((size, -1, held.shape[1])), axis, 0, 0, tiled=True)
        return add([parts[k] for k in range(size)])
    half = held.shape[0] // 2
    return add([held[:half], swap(held[half:], axis, way)])


def run(steps, do, held):
    for step in steps:
        if step == "b":
            held["i"], held["t"] = lax.optimization_barrier((held["i"], held["t"]))
        else:
            which, axis, way = step
            held[which] = do(held[which], axis, way)


def slots(which, names):
    core = lax.axis_index("core")
    here = {n: lax.axis_index(n) for n in names}
    both = []
    for c in (core, 1 - core):
        both.append([{n: c if n == "core" else here[n] for n in names}])
    for step in OUT:
        if step == "b" or step[0] != which:
            continue
        _, axis, way = step
        if axis == "core":
            both = [both[0] + both[1], both[1] + both[0]]
        elif way == "a":
            both = [[{**f, axis: jnp.int32(k)} for k in range(SIZES[AXES.index(axis)]) for f in b] for b in both]
        else:
            masks = [jnp.where(c == 0, way[0], way[1]) for c in (core, 1 - core)]
            both = [b + [{**f, axis: f[axis] ^ m} for f in b] for b, m in zip(both, masks)]
    blocks = []
    for f in both[0]:
        block = jnp.int32(0)
        for n in names:
            block = block * SIZES[AXES.index(n)] + f[n]
        blocks.append(block)
    return jnp.stack(blocks)


def unit_kernel(img_ref, txt_ref, img_out, txt_out):
    for src, dst in ((img_ref, img_out), (txt_ref, txt_out)):
        wide = src[...].astype(jnp.float32)
        length = jnp.sqrt(jnp.sum(wide * wide, axis=1, keepdims=True) + 1e-06)
        unit = wide / length
        dst[...] = jnp.concatenate([unit, jnp.zeros((PAD - ROWS, D), jnp.float32)]).astype(jnp.bfloat16)


def pair_kernel(scal_ref, img_ref, txt_ref, row_ref, col_ref, gimg_ref, gtxt_ref, w_ref):
    scale, bias = scal_ref[0], scal_ref[1]
    n = img_ref.shape[0]
    tile = 256
    for t in range(n // tile):
        rows = pl.ds(t * tile, tile)
        s = lax.dot_general(img_ref[rows, :], txt_ref[...], (((1,), (1,)), ((), ())), preferred_element_type=jnp.float32)
        z = scale * s + bias
        same = row_ref[rows, :] == col_ref[...]
        w = jnp.where(same, -1.0, 1.0) / (1.0 + jnp.exp(jnp.where(same, z, -z)))
        w_ref[rows, :] = w.astype(jnp.bfloat16)
    w_all = w_ref[...]
    for t in range(3):
        cols = pl.ds(t * 384, 384)
        g = lax.dot_general(w_all, img_ref[:, cols], (((0,), (0,)), ((), ())), preferred_element_type=jnp.float32)
        gtxt_ref[:, cols] = (scale * g).astype(jnp.bfloat16)
    for t in range(3):
        cols = pl.ds(t * 384, 384)
        g = jnp.dot(w_all, txt_ref[:, cols], preferred_element_type=jnp.float32)
        gimg_ref[:, cols] = (scale * g).astype(jnp.bfloat16)


def back_kernel(img_ref, txt_ref, gi_ref, gt_ref, img_out, txt_out):
    for src, g_ref, dst in ((img_ref, gi_ref, img_out), (txt_ref, gt_ref, txt_out)):
        wide = src[...].astype(jnp.float32)
        length = jnp.sqrt(jnp.sum(wide * wide, axis=1, keepdims=True) + 1e-06)
        unit = wide / length
        g = g_ref[...].astype(jnp.float32)[:ROWS]
        along = jnp.sum(unit * g, axis=1, keepdims=True)
        dst[...] = (g - unit * along) / length


def vm():
    return pl.BlockSpec(memory_space=pltpu.VMEM)


PARAMS = pltpu.CompilerParams(vmem_limit_bytes=VMEM)


def on_device(images, texts, logarithmic_scale, similarity_bias):
    block = jax.ShapeDtypeStruct((PAD, D), jnp.bfloat16)
    img, txt = pl.pallas_call(unit_kernel, out_shape=(block, block), in_specs=[vm()] * 2, out_specs=(vm(), vm()), compiler_params=PARAMS, name="unit")(images, texts)
    held = {"i": img, "t": txt}
    run(OUT, spread, held)
    img, txt = held["i"], held["t"]
    row = lax.axis_index("zh") * 4 + lax.axis_index("x")
    col = (lax.axis_index("zl") * 4 + lax.axis_index("y")) * 2 + lax.axis_index("core")
    img_ids = row * 32 + slots("i", ("zl", "y", "core"))
    txt_ids = col * 16 + slots("t", ("zh", "x"))
    within = jnp.arange(PAD, dtype=jnp.int32)
    row_ids = jnp.where(within < ROWS, img_ids[:, None] * ROWS + within, -1).reshape(-1, 1)
    col_ids = jnp.where(within < ROWS, txt_ids[:, None] * ROWS + within, -2).reshape(1, -1)
    scal = jnp.stack([jnp.exp(logarithmic_scale), similarity_bias])
    ni, nt = img.shape[0], txt.shape[0]
    gimg, gtxt = pl.pallas_call(
        pair_kernel,
        out_shape=(jax.ShapeDtypeStruct((ni, D), jnp.bfloat16), jax.ShapeDtypeStruct((nt, D), jnp.bfloat16)),
        in_specs=[pl.BlockSpec(memory_space=pltpu.SMEM)] + [vm()] * 4,
        out_specs=(vm(), vm()),
        scratch_shapes=[pltpu.VMEM((ni, nt), jnp.bfloat16)],
        compiler_params=PARAMS,
        name="pairs",
    )(scal, img, txt, row_ids, col_ids)
    held = {"i": gimg, "t": gtxt}
    run(BACK, collect, held)
    gimg, gtxt = held["i"], held["t"]
    wide = jax.ShapeDtypeStruct((ROWS, D), jnp.float32)
    return pl.pallas_call(back_kernel, out_shape=(wide, wide), in_specs=[vm()] * 4, out_specs=(vm(), vm()), compiler_params=PARAMS, name="back")(images, texts, gimg, gtxt)


def solution(mesh):
    fine = Mesh(mesh.devices.reshape(SIZES), AXES)
    return jax.shard_map(
        on_device,
        mesh=fine,
        in_specs=(P(AXES, None), P(("zl", "y", "core", "zh", "x"), None), P(), P()),
        out_specs=(P(AXES, None), P(("zl", "y", "core", "zh", "x"), None)),
        check_vma=False,
    )
```

```python
import functools

import jax
import jax.numpy as jnp
from jax import lax
from jax.experimental import pallas as pl
from jax.experimental.pallas import tpu as pltpu
from jax.sharding import Mesh
from jax.sharding import PartitionSpec as P

D = 1152
ROWS = 22
PAD = 24
AXES = ("zh", "x", "zl", "y", "core")
SIZES = (4, 4, 4, 4, 2)
VMEM = 48 * 1024 * 1024
def at_z(move):
    return lambda p: {**p, "z": move(p["z"])}


def at_y(mask):
    return lambda p: {**p, "y": p["y"] ^ mask}


def at_x(mask):
    return lambda p: {**p, "x": p["x"] ^ mask}


FAR = (at_z(lambda z: z ^ 4), at_z(lambda z: z ^ 12))
NEAR = (at_z(lambda z: z ^ 1), at_z(lambda z: z ^ 2))
BOTH = (at_z(lambda z: z ^ 5), at_z(lambda z: z ^ 14))
LAST = tuple((at_y(m), at_x(m)) for m in (1, 3, 2))
ROUNDS = ((FAR, NEAR, BOTH), LAST)
BACK = ((FAR,), (NEAR,))


def flat(zh, x, zl, y, core):
    return (((zh * 4 + x) * 4 + zl) * 4 + y) * 2 + core


def fetch(value, sources, back=False):
    pairs = []
    for z in range(16):
        for x in range(4):
            for y in range(4):
                for c in range(2):
                    at = {"x": x, "y": y, "z": z}
                    pairs.append(tuple(flat(p["z"] >> 2, p["x"], p["z"] & 3, p["y"], c) for p in (sources[c](at), at)))
    return lax.ppermute(value, AXES, [(b, a) for a, b in pairs] if back else pairs)


def core_swap(value):
    return lax.ppermute(value, "core", [(0, 1), (1, 0)])


def add(parts):
    return sum(p.astype(jnp.float32) for p in parts).astype(jnp.bfloat16)


def origins(at, core):
    found = [at]
    for sources in reversed(ROUNDS):
        found = [q for p in found for q in [p] + [s[core](p) for s in sources]]
    return [{**p, "core": c} for p in found for c in (core, 1 - core)]


def unit_of(ref):
    wide = ref[...].astype(jnp.float32)
    length = jnp.sqrt(jnp.sum(wide * wide, axis=1, keepdims=True) + 1e-06)
    return wide / length, length


def unit_kernel(core_ref, img_ref, txt_ref, keep_ref, send_ref):
    pad = jnp.zeros((PAD - ROWS, D), jnp.float32)
    img, txt = (jnp.concatenate([unit_of(ref)[0], pad]).astype(jnp.bfloat16) for ref in (img_ref, txt_ref))

    @pl.when(core_ref[0] == 0)
    def _():
        keep_ref[...] = img
        send_ref[...] = txt

    @pl.when(core_ref[0] == 1)
    def _():
        keep_ref[...] = txt
        send_ref[...] = img


def row_ids(ids_ref, first, count):
    within = lax.broadcasted_iota(jnp.int32, (PAD, 1), 0)
    return jnp.concatenate([jnp.where(within < ROWS, ids_ref[first + k] * ROWS + within, -1) for k in range(count)])


def column_ids(ids_ref, first, count):
    at = lax.broadcasted_iota(jnp.int32, (1, count * PAD), 1)
    found = jnp.full(at.shape, -2, jnp.int32)
    for k in range(count):
        within = at - k * PAD
        found = jnp.where((within >= 0) & (within < ROWS), ids_ref[first + k] * ROWS + within, found)
    return found


def pair_kernel(scal_ref, mine_ids, their_ids, me_ref, ml_ref, re_ref, rl_ref, *outs):
    scale, bias = scal_ref[0], scal_ref[1]
    half = me_ref.shape[0] // 2
    slots = me_ref.shape[0] // PAD
    theirs = [(ref, column_ids(their_ids, k * slots, slots)) for k, ref in enumerate((re_ref, rl_ref))]
    for k, mine_ref in enumerate((me_ref, ml_ref)):
        rows = row_ids(mine_ids, k * slots, slots)
        weights = []
        for their_ref, columns in theirs:
            s = lax.dot_general(mine_ref[...], their_ref[...], (((1,), (1,)), ((), ())), preferred_element_type=jnp.float32)
            z = scale * s + bias
            same = rows == columns
            d = 1.0 + jnp.exp(jnp.where(same, z, -z))
            r = pl.reciprocal(d, approx=True)
            r = r * (2.0 - d * r)
            weights.append(jnp.where(same, -r, r).astype(jnp.bfloat16))
        for t in range(3):
            cols = pl.ds(t * 384, 384)
            g = sum(jnp.dot(w, ref[:, cols], preferred_element_type=jnp.float32) for w, (ref, _) in zip(weights, theirs))
            g = (scale * g).astype(jnp.bfloat16)
            outs[2 * k][:, cols] = g[:half]
            outs[2 * k + 1][:, cols] = g[half:]


def back_kernel(core_ref, img_ref, txt_ref, *refs):
    *mine, recv_ref, img_out, txt_out = refs

    def work(own_src, own_out, other_src, other_out):
        own = sum(ref[...].astype(jnp.float32) for ref in mine)
        for src, g, dst in ((own_src, own, own_out), (other_src, recv_ref[...].astype(jnp.float32), other_out)):
            unit, length = unit_of(src)
            g = g[:ROWS]
            along = jnp.sum(unit * g, axis=1, keepdims=True)
            dst[...] = (g - unit * along) / length

    pl.when(core_ref[0] == 0)(lambda: work(img_ref, img_out, txt_ref, txt_out))
    pl.when(core_ref[0] == 1)(lambda: work(txt_ref, txt_out, img_ref, img_out))


PARAMS = pltpu.CompilerParams(vmem_limit_bytes=VMEM)


def call(kernel, name, out_shape, scalars, args, flops=0):
    return pl.pallas_call(
        kernel,
        out_shape=out_shape,
        in_specs=[pl.BlockSpec(memory_space=pltpu.SMEM)] * len(scalars) + [pl.BlockSpec(memory_space=pltpu.VMEM)] * len(args),
        out_specs=tuple(pl.BlockSpec(memory_space=pltpu.VMEM) for _ in out_shape),
        compiler_params=PARAMS,
        cost_estimate=pl.CostEstimate(flops=flops, bytes_accessed=1 << 20, transcendentals=0),
        name=name,
    )(*scalars, *args)


def on_device(images, texts, logarithmic_scale, similarity_bias):
    core = lax.axis_index("core")
    at = {"x": lax.axis_index("x"), "y": lax.axis_index("y"), "z": lax.axis_index("zh") * 4 + lax.axis_index("zl")}
    cores = core.reshape((1,))
    block = jax.ShapeDtypeStruct((PAD, D), jnp.bfloat16)
    keep, send = call(unit_kernel, "unit", (block, block), [cores], [images, texts])
    held = jnp.concatenate([keep, core_swap(send)])
    for sources in ROUNDS[:-1]:
        held = jnp.concatenate([held] + [fetch(held, s) for s in sources])
    first, second, third = [fetch(held, s) for s in ROUNDS[-1]]
    me = jnp.concatenate([held, first])
    ml = jnp.concatenate([second, third])
    re, rl = core_swap(me), core_swap(ml)

    img_ids = jnp.stack([((p["z"] >> 2) * 4 + p["x"]) * 32 + ((p["z"] & 3) * 4 + p["y"]) * 2 + p["core"] for p in origins(at, 0)])
    txt_ids = jnp.stack([(((p["z"] & 3) * 4 + p["y"]) * 2 + p["core"]) * 16 + (p["z"] >> 2) * 4 + p["x"] for p in origins(at, 1)])
    mine_ids, their_ids = jnp.where(core == 0, img_ids, txt_ids), jnp.where(core == 0, txt_ids, img_ids)
    scal = jnp.stack([jnp.exp(logarithmic_scale), similarity_bias])
    n = me.shape[0]
    piece = jax.ShapeDtypeStruct((n // 2, D), jnp.bfloat16)
    keep, *sends = call(pair_kernel, "pairs", (piece,) * 4, [scal, mine_ids, their_ids], [me, ml, re, rl], 16 * n * n * D)
    parts = [keep] + [fetch(p, s, True) for p, s in zip(sends, ROUNDS[-1])]
    for sources in reversed(BACK):
        n = parts[0].shape[0] // (len(sources) + 1)
        sends = [add([p[k * n : (k + 1) * n] for p in parts]) for k in range(1, len(sources) + 1)]
        parts = [p[:n] for p in parts] + [fetch(p, s, True) for p, s in zip(sends, sources)]
    recv = core_swap(add([p[PAD:] for p in parts]))
    wide = jax.ShapeDtypeStruct((ROWS, D), jnp.float32)
    return call(back_kernel, "back", (wide, wide), [cores], [images, texts] + [p[:PAD] for p in parts] + [recv])


def solution(mesh):
    fine = Mesh(mesh.devices.reshape(SIZES), AXES)
    return jax.shard_map(
        on_device,
        mesh=fine,
        in_specs=(P(AXES, None), P(("zl", "y", "core", "zh", "x"), None), P(), P()),
        out_specs=(P(AXES, None), P(("zl", "y", "core", "zh", "x"), None)),
        check_vma=False,
    )
```

```python
import functools

import jax
import jax.numpy as jnp
import numpy as np
from jax import lax
from jax.experimental import pallas as pl
from jax.experimental.pallas import tpu as pltpu
from jax.sharding import Mesh
from jax.sharding import PartitionSpec as P

D = 1152
ROWS = 22
PAD = 24
AXES = ("zh", "x", "zl", "y", "core")
SIZES = (4, 4, 4, 4, 2)
VMEM = 16 * 1024 * 1024
def at_z(move):
    return lambda p: {**p, "z": move(p["z"])}


def at_y(mask):
    return lambda p: {**p, "y": p["y"] ^ mask}


def at_x(mask):
    return lambda p: {**p, "x": p["x"] ^ mask}


FAR = (at_z(lambda z: z ^ 4), at_z(lambda z: z ^ 12))
NEAR = (at_z(lambda z: z ^ 1), at_z(lambda z: z ^ 2))
BOTH = (at_z(lambda z: z ^ 5), at_z(lambda z: z ^ 14))
LAST = tuple((at_y(m), at_x(m)) for m in (1, 3, 2))
ROUNDS = ((FAR, NEAR, BOTH), LAST)
BACK = ((FAR,), (NEAR,))


def flat(zh, x, zl, y, core):
    return (((zh * 4 + x) * 4 + zl) * 4 + y) * 2 + core


def fetch(value, sources, back=False):
    pairs = []
    for z in range(16):
        for x in range(4):
            for y in range(4):
                for c in range(2):
                    at = {"x": x, "y": y, "z": z}
                    pairs.append(tuple(flat(p["z"] >> 2, p["x"], p["z"] & 3, p["y"], c) for p in (sources[c](at), at)))
    return lax.ppermute(value, AXES, [(b, a) for a, b in pairs] if back else pairs)


def core_swap(value):
    return lax.ppermute(value, "core", [(0, 1), (1, 0)])


def add(parts):
    return sum(p.astype(jnp.float32) for p in parts).astype(jnp.bfloat16)


def blocks_of(place_ref, mine):
    x, y, z, core = (place_ref[k] for k in range(4))
    images = core == 0 if mine else core == 1

    def first(mask):
        zi, zt = z ^ mask[0], z ^ mask[1]
        return jnp.where(images, (zi >> 2) * 128 + (zi & 3) * 8, (zt & 3) * 128 + (zt >> 2) * 4)

    firsts = [first(mask) for mask in ((0, 0), (4, 12), (1, 2), (5, 14))]
    lasts = [jnp.where(images, x * 32 + (y ^ m) * 2, y * 32 + (x ^ m)) for m in (0, 1, 3, 2)]
    sides = [jnp.where(images, k, (1 - k) * 16) for k in range(2)]
    return lasts, firsts, sides


def cat_kernel(core_ref, both_ref, keep_ref, send_ref):
    img, txt = (unit_of(both_ref[k])[0].astype(jnp.bfloat16) for k in range(2))

    @pl.when(core_ref[0] == 0)
    def _():
        keep_ref[...] = img
        send_ref[...] = txt

    @pl.when(core_ref[0] == 1)
    def _():
        keep_ref[...] = txt
        send_ref[...] = img


def row_ids(blocks, start, stop):
    within = lax.broadcasted_iota(jnp.int32, (PAD, 1), 0)
    lasts, firsts, sides = blocks
    ids = [a + b + c for a in lasts[start:stop] for b in firsts for c in sides]
    return jnp.concatenate([jnp.where(within < ROWS, k * ROWS + within, -1) for k in ids])


def column_ids(blocks, start, stop):
    lasts, firsts, sides = blocks
    ids = [a + b + c for a in lasts[start:stop] for b in firsts for c in sides]
    at = lax.broadcasted_iota(jnp.int32, (1, len(ids) * PAD), 1)
    found = jnp.full(at.shape, -2, jnp.int32)
    for k, block in enumerate(ids):
        within = at - k * PAD
        found = jnp.where((within >= 0) & (within < ROWS), block * ROWS + within, found)
    return found


def unit_of(wide):
    wide = wide.astype(jnp.float32)
    length = jnp.sqrt(jnp.sum(wide * wide, axis=1, keepdims=True) + 1e-06)
    return wide / length, length


def unit_kernel(core_ref, both_ref, keep_ref, send_ref):
    img, txt = (unit_of(both_ref[k])[0].astype(jnp.bfloat16) for k in range(2))

    @pl.when(core_ref[0] == 0)
    def _():
        keep_ref[...] = img
        send_ref[...] = txt

    @pl.when(core_ref[0] == 1)
    def _():
        keep_ref[...] = txt
        send_ref[...] = img


def row_ids(blocks, start, stop):
    within = lax.broadcasted_iota(jnp.int32, (PAD, 1), 0)
    lasts, firsts, sides = blocks
    ids = [a + b + c for a in lasts[start:stop] for b in firsts for c in sides]
    return jnp.concatenate([jnp.where(within < ROWS, k * ROWS + within, -1) for k in ids])


def column_ids(blocks, start, stop):
    lasts, firsts, sides = blocks
    ids = [a + b + c for a in lasts[start:stop] for b in firsts for c in sides]
    at = lax.broadcasted_iota(jnp.int32, (1, len(ids) * PAD), 1)
    found = jnp.full(at.shape, -2, jnp.int32)
    for k, block in enumerate(ids):
        within = at - k * PAD
        found = jnp.where((within >= 0) & (within < ROWS), block * ROWS + within, found)
    return found


def unit_of(wide):
    wide = wide.astype(jnp.float32)
    length = jnp.sqrt(jnp.sum(wide * wide, axis=1, keepdims=True) + 1e-06)
    return wide / length, length


def weights_of(scal_ref, rows, columns, mine_ref, their_ref):
    s = lax.dot_general(mine_ref[...], their_ref[...], (((1,), (1,)), ((), ())), preferred_element_type=jnp.float32)
    label = jnp.where(rows == columns, 1.0, -1.0)
    d = 1.0 + jnp.exp(label * (scal_ref[0] * s + scal_ref[1]))
    r = pl.reciprocal(d, approx=True)
    r = r * (2.0 - d * r)
    return (-label * r).astype(jnp.bfloat16)


def pair_kernel(scal_ref, place_ref, me_ref, ml_ref, re_ref, rl_ref, *refs):
    *outs, their_ref = refs
    n = me_ref.shape[0]
    their_ref[:n, :] = re_ref[...]
    their_ref[n:, :] = rl_ref[...]
    mine_blocks, their_blocks = blocks_of(place_ref, True), blocks_of(place_ref, False)
    columns = column_ids(their_blocks, 0, 4)
    halves = [
        (k, weights_of(scal_ref, row_ids(mine_blocks, 2 * k, 2 * k + 2), columns, mine_ref, their_ref))
        for k, mine_ref in ((1, ml_ref), (0, me_ref))
    ]
    for k, w in halves:
        for t in range(3):
            cols = pl.ds(t * 384, 384)
            g = (scal_ref[0] * jnp.dot(w, their_ref[:, cols], preferred_element_type=jnp.float32)).astype(jnp.bfloat16)
            outs[2 * k][:, cols] = g[: n // 2]
            outs[2 * k + 1][:, cols] = g[n // 2 :]


def back_kernel(core_ref, img_ref, txt_ref, *refs):
    *mine, recv_ref, img_out, txt_out = refs

    def work(own_src, own_out, other_src, other_out):
        own = sum(ref[...].astype(jnp.float32) for ref in mine)
        for src, g, dst in ((own_src, own, own_out), (other_src, recv_ref[...].astype(jnp.float32), other_out)):
            unit, length = unit_of(src[...])
            g = g[:ROWS]
            along = jnp.sum(unit * g, axis=1, keepdims=True)
            dst[...] = (g - unit * along) / length

    pl.when(core_ref[0] == 0)(lambda: work(img_ref, img_out, txt_ref, txt_out))
    pl.when(core_ref[0] == 1)(lambda: work(txt_ref, txt_out, img_ref, img_out))


def call(kernel, name, out_shape, scalars, args, flops=0, scratch=()):
    vmem = pl.BlockSpec(memory_space=pltpu.VMEM)
    return pl.pallas_call(
        kernel,
        out_shape=out_shape,
        scratch_shapes=list(scratch),
        in_specs=[pl.BlockSpec(memory_space=pltpu.SMEM)] * len(scalars) + [vmem] * len(args),
        out_specs=(vmem,) * len(out_shape),
        compiler_params=pltpu.CompilerParams(vmem_limit_bytes=VMEM),
        cost_estimate=pl.CostEstimate(flops=flops, bytes_accessed=1 << 20, transcendentals=0),
        name=name,
    )(*scalars, *args)


def on_device(images, texts, logarithmic_scale, similarity_bias):
    core = lax.axis_index("core")
    place = jnp.stack([lax.axis_index("x"), lax.axis_index("y"), lax.axis_index("zh") * 4 + lax.axis_index("zl"), core])
    scal = jnp.stack([jnp.exp(logarithmic_scale), similarity_bias])
    cores = core.reshape((1,))
    block = jax.ShapeDtypeStruct((PAD, D), jnp.bfloat16)
    both = jnp.stack([jnp.pad(v, ((0, PAD - ROWS), (0, 0))) for v in (images, texts)])
    keep, send = call(unit_kernel, "unit", (block, block), [cores], [both])
    held = jnp.concatenate([keep, core_swap(send)])
    for sources in ROUNDS[:-1]:
        held = jnp.concatenate([held] + [fetch(held, s) for s in sources])
    one, three, two = [fetch(held, s) for s in ROUNDS[-1]]
    me = jnp.concatenate([held, one])
    re = core_swap(me)
    scalars = [scal, place]
    n = me.shape[0]
    piece = jax.ShapeDtypeStruct((n // 2, D), jnp.bfloat16)
    flops = 4 * n * n * D

    ml = jnp.concatenate([three, two])
    rl = core_swap(ml)
    keep, p1, p3, p2 = call(
        pair_kernel, "pairs", (piece,) * 4, scalars, [me, ml, re, rl], 4 * flops, [pltpu.VMEM((2 * n, D), jnp.bfloat16)]
    )
    parts = [keep] + [fetch(p, s, True) for p, s in zip((p1, p3, p2), LAST)]
    for sources in reversed(BACK):
        n = parts[0].shape[0] // (len(sources) + 1)
        sends = [add([p[k * n : (k + 1) * n] for p in parts]) for k in range(1, len(sources) + 1)]
        parts = [p[:n] for p in parts] + [fetch(p, s, True) for p, s in zip(sends, sources)]
    recv = core_swap(add([p[PAD:] for p in parts]))
    wide = jax.ShapeDtypeStruct((ROWS, D), jnp.float32)
    return call(back_kernel, "back", (wide, wide), [cores], [images, texts] + [p[:PAD] for p in parts] + [recv])


def solution(mesh):
    fine = Mesh(mesh.devices.reshape(SIZES), AXES)
    return jax.shard_map(
        on_device,
        mesh=fine,
        in_specs=(P(AXES, None), P(("zl", "y", "core", "zh", "x"), None), P(), P()),
        out_specs=(P(AXES, None), P(("zl", "y", "core", "zh", "x"), None)),
        check_vma=False,
    )
```

```python
import functools

import jax
import jax.numpy as jnp
import numpy as np
from jax import lax
from jax.experimental import pallas as pl
from jax.experimental.pallas import tpu as pltpu
from jax.sharding import Mesh
from jax.sharding import PartitionSpec as P

D = 1152
ROWS = 22
PAD = 24
AXES = ("zh", "x", "zl", "y", "core")
SIZES = (4, 4, 4, 4, 2)
VMEM = 16 * 1024 * 1024
def at_z(move):
    return lambda p: {**p, "z": move(p["z"])}


def at_y(mask):
    return lambda p: {**p, "y": p["y"] ^ mask}


def at_x(mask):
    return lambda p: {**p, "x": p["x"] ^ mask}


FAR = (at_z(lambda z: z ^ 4), at_z(lambda z: z ^ 12))
NEAR = (at_z(lambda z: z ^ 1), at_z(lambda z: z ^ 2))
BOTH = (at_z(lambda z: z ^ 5), at_z(lambda z: z ^ 14))
LAST = tuple((at_y(m), at_x(m)) for m in (1, 3, 2))
ROUNDS = ((FAR, NEAR, BOTH), LAST)
BACK = ((FAR,), (NEAR,))


def flat(zh, x, zl, y, core):
    return (((zh * 4 + x) * 4 + zl) * 4 + y) * 2 + core


def fetch(value, sources, back=False):
    pairs = []
    for z in range(16):
        for x in range(4):
            for y in range(4):
                for c in range(2):
                    at = {"x": x, "y": y, "z": z}
                    pairs.append(tuple(flat(p["z"] >> 2, p["x"], p["z"] & 3, p["y"], c) for p in (sources[c](at), at)))
    return lax.ppermute(value, AXES, [(b, a) for a, b in pairs] if back else pairs)


def core_swap(value):
    return lax.ppermute(value, "core", [(0, 1), (1, 0)])


def add(parts):
    return sum(p.astype(jnp.float32) for p in parts).astype(jnp.bfloat16)


def blocks_of(place_ref, mine):
    x, y, z, core = (place_ref[k] for k in range(4))
    images = core == 0 if mine else core == 1

    def first(mask):
        zi, zt = z ^ mask[0], z ^ mask[1]
        return jnp.where(images, (zi >> 2) * 128 + (zi & 3) * 8, (zt & 3) * 128 + (zt >> 2) * 4)

    firsts = [first(mask) for mask in ((0, 0), (4, 12), (1, 2), (5, 14))]
    lasts = [jnp.where(images, x * 32 + (y ^ m) * 2, y * 32 + (x ^ m)) for m in (0, 1, 3, 2)]
    sides = [jnp.where(images, k, (1 - k) * 16) for k in range(2)]
    return lasts, firsts, sides


def cat_kernel(core_ref, both_ref, keep_ref, send_ref):
    img, txt = (unit_of(both_ref[k])[0].astype(jnp.bfloat16) for k in range(2))

    @pl.when(core_ref[0] == 0)
    def _():
        keep_ref[...] = img
        send_ref[...] = txt

    @pl.when(core_ref[0] == 1)
    def _():
        keep_ref[...] = txt
        send_ref[...] = img


def row_ids(blocks, start, stop):
    within = lax.broadcasted_iota(jnp.int32, (PAD, 1), 0)
    lasts, firsts, sides = blocks
    ids = [a + b + c for a in lasts[start:stop] for b in firsts for c in sides]
    return jnp.concatenate([jnp.where(within < ROWS, k * ROWS + within, -1) for k in ids])


def column_ids(blocks, start, stop):
    lasts, firsts, sides = blocks
    ids = [a + b + c for a in lasts[start:stop] for b in firsts for c in sides]
    at = lax.broadcasted_iota(jnp.int32, (1, len(ids) * PAD), 1)
    found = jnp.full(at.shape, -2, jnp.int32)
    for k, block in enumerate(ids):
        within = at - k * PAD
        found = jnp.where((within >= 0) & (within < ROWS), block * ROWS + within, found)
    return found


def unit_of(wide):
    wide = wide.astype(jnp.float32)
    length = jnp.sqrt(jnp.sum(wide * wide, axis=1, keepdims=True) + 1e-06)
    return wide / length, length


def unit_kernel(core_ref, both_ref, keep_ref, send_ref):
    img, txt = (unit_of(both_ref[k])[0].astype(jnp.bfloat16) for k in range(2))

    @pl.when(core_ref[0] == 0)
    def _():
        keep_ref[...] = img
        send_ref[...] = txt

    @pl.when(core_ref[0] == 1)
    def _():
        keep_ref[...] = txt
        send_ref[...] = img


def row_ids(blocks, start, stop):
    within = lax.broadcasted_iota(jnp.int32, (PAD, 1), 0)
    lasts, firsts, sides = blocks
    ids = [a + b + c for a in lasts[start:stop] for b in firsts for c in sides]
    return jnp.concatenate([jnp.where(within < ROWS, k * ROWS + within, -1) for k in ids])


def column_ids(blocks, start, stop):
    lasts, firsts, sides = blocks
    ids = [a + b + c for a in lasts[start:stop] for b in firsts for c in sides]
    at = lax.broadcasted_iota(jnp.int32, (1, len(ids) * PAD), 1)
    found = jnp.full(at.shape, -2, jnp.int32)
    for k, block in enumerate(ids):
        within = at - k * PAD
        found = jnp.where((within >= 0) & (within < ROWS), block * ROWS + within, found)
    return found


def unit_of(wide):
    wide = wide.astype(jnp.float32)
    length = jnp.sqrt(jnp.sum(wide * wide, axis=1, keepdims=True) + 1e-06)
    return wide / length, length


def weights_of(scal_ref, rows, columns, mine_ref, their_ref):
    s = lax.dot_general(mine_ref[...], their_ref[...], (((1,), (1,)), ((), ())), preferred_element_type=jnp.float32)
    label = jnp.where(rows == columns, 1.0, -1.0)
    d = 1.0 + jnp.exp(label * (scal_ref[0] * s + scal_ref[1]))
    r = pl.reciprocal(d, approx=True)
    r = r * (2.0 - d * r)
    return (-label * r).astype(jnp.bfloat16)


def pair_kernel(scal_ref, place_ref, me_ref, ml_ref, re_ref, rl_ref, *refs):
    *outs, their_ref = refs
    n = me_ref.shape[0]
    their_ref[:n, :] = re_ref[...]
    their_ref[n:, :] = rl_ref[...]
    mine_blocks, their_blocks = blocks_of(place_ref, True), blocks_of(place_ref, False)
    columns = column_ids(their_blocks, 0, 4)
    halves = [
        (k, weights_of(scal_ref, row_ids(mine_blocks, 2 * k, 2 * k + 2), columns, mine_ref, their_ref))
        for k, mine_ref in ((1, ml_ref), (0, me_ref))
    ]
    for k, w in halves:
        for start, width in ((0, 512), (512, 512), (1024, 128)):
            cols = pl.ds(start, width)
            g = (scal_ref[0] * jnp.dot(w, their_ref[:, cols], preferred_element_type=jnp.float32)).astype(jnp.bfloat16)
            outs[2 * k][:, cols] = g[: n // 2]
            outs[2 * k + 1][:, cols] = g[n // 2 :]


def back_kernel(core_ref, img_ref, txt_ref, *refs):
    *mine, recv_ref, img_out, txt_out = refs

    def work(own_src, own_out, other_src, other_out):
        own = sum(ref[...].astype(jnp.float32) for ref in mine)
        for src, g, dst in ((own_src, own, own_out), (other_src, recv_ref[...].astype(jnp.float32), other_out)):
            unit, length = unit_of(src[...])
            g = g[:ROWS]
            along = jnp.sum(unit * g, axis=1, keepdims=True)
            dst[...] = (g - unit * along) / length

    pl.when(core_ref[0] == 0)(lambda: work(img_ref, img_out, txt_ref, txt_out))
    pl.when(core_ref[0] == 1)(lambda: work(txt_ref, txt_out, img_ref, img_out))


def call(kernel, name, out_shape, scalars, args, flops=0, scratch=()):
    vmem = pl.BlockSpec(memory_space=pltpu.VMEM)
    return pl.pallas_call(
        kernel,
        out_shape=out_shape,
        scratch_shapes=list(scratch),
        in_specs=[pl.BlockSpec(memory_space=pltpu.SMEM)] * len(scalars) + [vmem] * len(args),
        out_specs=(vmem,) * len(out_shape),
        compiler_params=pltpu.CompilerParams(vmem_limit_bytes=VMEM),
        cost_estimate=pl.CostEstimate(flops=flops, bytes_accessed=1 << 20, transcendentals=0),
        name=name,
    )(*scalars, *args)


def on_device(images, texts, logarithmic_scale, similarity_bias):
    core = lax.axis_index("core")
    place = jnp.stack([lax.axis_index("x"), lax.axis_index("y"), lax.axis_index("zh") * 4 + lax.axis_index("zl"), core])
    scal = jnp.stack([jnp.exp(logarithmic_scale), similarity_bias])
    cores = core.reshape((1,))
    block = jax.ShapeDtypeStruct((PAD, D), jnp.bfloat16)
    both = jnp.stack([jnp.pad(v, ((0, PAD - ROWS), (0, 0))) for v in (images, texts)])
    keep, send = call(unit_kernel, "unit", (block, block), [cores], [both])
    held = jnp.concatenate([keep, core_swap(send)])
    for sources in ROUNDS[:-1]:
        held = jnp.concatenate([held] + [fetch(held, s) for s in sources])
    one, three, two = [fetch(held, s) for s in ROUNDS[-1]]
    me = jnp.concatenate([held, one])
    re = core_swap(me)
    scalars = [scal, place]
    n = me.shape[0]
    piece = jax.ShapeDtypeStruct((n // 2, D), jnp.bfloat16)
    flops = 4 * n * n * D

    ml = jnp.concatenate([three, two])
    rl = core_swap(ml)
    keep, p1, p3, p2 = call(
        pair_kernel, "pairs", (piece,) * 4, scalars, [me, ml, re, rl], 4 * flops, [pltpu.VMEM((2 * n, D), jnp.bfloat16)]
    )
    parts = [keep] + [fetch(p, s, True) for p, s in zip((p1, p3, p2), LAST)]
    for sources in reversed(BACK):
        n = parts[0].shape[0] // (len(sources) + 1)
        sends = [add([p[k * n : (k + 1) * n] for p in parts]) for k in range(1, len(sources) + 1)]
        parts = [p[:n] for p in parts] + [fetch(p, s, True) for p, s in zip(sends, sources)]
    recv = core_swap(add([p[PAD:] for p in parts]))
    wide = jax.ShapeDtypeStruct((ROWS, D), jnp.float32)
    return call(back_kernel, "back", (wide, wide), [cores], [images, texts] + [p[:PAD] for p in parts] + [recv])


def solution(mesh):
    fine = Mesh(mesh.devices.reshape(SIZES), AXES)
    return jax.shard_map(
        on_device,
        mesh=fine,
        in_specs=(P(AXES, None), P(("zl", "y", "core", "zh", "x"), None), P(), P()),
        out_specs=(P(AXES, None), P(("zl", "y", "core", "zh", "x"), None)),
        check_vma=False,
    )
```

```python
import functools

import jax
import jax.numpy as jnp
import numpy as np
from jax import lax
from jax.experimental import pallas as pl
from jax.experimental.pallas import tpu as pltpu
from jax.sharding import Mesh
from jax.sharding import PartitionSpec as P

D = 1152
ROWS = 22
PAD = 24
AXES = ("zh", "x", "zl", "y", "core")
SIZES = (4, 4, 4, 4, 2)
VMEM = 16 * 1024 * 1024
def at_z(move):
    return lambda p: {**p, "z": move(p["z"])}


def at_y(mask):
    return lambda p: {**p, "y": p["y"] ^ mask}


def at_x(mask):
    return lambda p: {**p, "x": p["x"] ^ mask}


FAR = (at_z(lambda z: z ^ 4), at_z(lambda z: z ^ 12))
NEAR = (at_z(lambda z: z ^ 1), at_z(lambda z: z ^ 2))
BOTH = (at_z(lambda z: z ^ 5), at_z(lambda z: z ^ 14))
LAST = tuple((at_y(m), at_x(m)) for m in (1, 3, 2))
ROUNDS = ((FAR, NEAR, BOTH), LAST)
BACK = ((FAR,), (NEAR,))


def flat(zh, x, zl, y, core):
    return (((zh * 4 + x) * 4 + zl) * 4 + y) * 2 + core


def fetch(value, sources, back=False):
    pairs = []
    for z in range(16):
        for x in range(4):
            for y in range(4):
                for c in range(2):
                    at = {"x": x, "y": y, "z": z}
                    pairs.append(tuple(flat(p["z"] >> 2, p["x"], p["z"] & 3, p["y"], c) for p in (sources[c](at), at)))
    return lax.ppermute(value, AXES, [(b, a) for a, b in pairs] if back else pairs)


def core_swap(value):
    return lax.ppermute(value, "core", [(0, 1), (1, 0)])


def add(parts):
    return sum(p.astype(jnp.float32) for p in parts).astype(jnp.bfloat16)


def blocks_of(place_ref, mine):
    x, y, z, core = (place_ref[k] for k in range(4))
    images = core == 0 if mine else core == 1

    def first(mask):
        zi, zt = z ^ mask[0], z ^ mask[1]
        return jnp.where(images, (zi >> 2) * 128 + (zi & 3) * 8, (zt & 3) * 128 + (zt >> 2) * 4)

    firsts = [first(mask) for mask in ((0, 0), (4, 12), (1, 2), (5, 14))]
    lasts = [jnp.where(images, x * 32 + (y ^ m) * 2, y * 32 + (x ^ m)) for m in (0, 1, 3, 2)]
    sides = [jnp.where(images, k, (1 - k) * 16) for k in range(2)]
    return lasts, firsts, sides


def cat_kernel(core_ref, both_ref, keep_ref, send_ref):
    img, txt = (unit_of(both_ref[k])[0].astype(jnp.bfloat16) for k in range(2))

    @pl.when(core_ref[0] == 0)
    def _():
        keep_ref[...] = img
        send_ref[...] = txt

    @pl.when(core_ref[0] == 1)
    def _():
        keep_ref[...] = txt
        send_ref[...] = img


def row_ids(blocks, start, stop):
    within = lax.broadcasted_iota(jnp.int32, (PAD, 1), 0)
    lasts, firsts, sides = blocks
    ids = [a + b + c for a in lasts[start:stop] for b in firsts for c in sides]
    return jnp.concatenate([jnp.where(within < ROWS, k * ROWS + within, -1) for k in ids])


def column_ids(blocks, start, stop):
    lasts, firsts, sides = blocks
    ids = [a + b + c for a in lasts[start:stop] for b in firsts for c in sides]
    at = lax.broadcasted_iota(jnp.int32, (1, len(ids) * PAD), 1)
    found = jnp.full(at.shape, -2, jnp.int32)
    for k, block in enumerate(ids):
        within = at - k * PAD
        found = jnp.where((within >= 0) & (within < ROWS), block * ROWS + within, found)
    return found


def unit_of(wide):
    wide = wide.astype(jnp.float32)
    length = jnp.sqrt(jnp.sum(wide * wide, axis=1, keepdims=True) + 1e-06)
    return wide / length, length


def unit_kernel(core_ref, both_ref, keep_ref, send_ref):
    img, txt = (unit_of(both_ref[k])[0].astype(jnp.bfloat16) for k in range(2))

    @pl.when(core_ref[0] == 0)
    def _():
        keep_ref[...] = img
        send_ref[...] = txt

    @pl.when(core_ref[0] == 1)
    def _():
        keep_ref[...] = txt
        send_ref[...] = img


def row_ids(blocks, start, stop):
    within = lax.broadcasted_iota(jnp.int32, (PAD, 1), 0)
    lasts, firsts, sides = blocks
    ids = [a + b + c for a in lasts[start:stop] for b in firsts for c in sides]
    return jnp.concatenate([jnp.where(within < ROWS, k * ROWS + within, -1) for k in ids])


def column_ids(blocks, start, stop):
    lasts, firsts, sides = blocks
    ids = [a + b + c for a in lasts[start:stop] for b in firsts for c in sides]
    at = lax.broadcasted_iota(jnp.int32, (1, len(ids) * PAD), 1)
    found = jnp.full(at.shape, -2, jnp.int32)
    for k, block in enumerate(ids):
        within = at - k * PAD
        found = jnp.where((within >= 0) & (within < ROWS), block * ROWS + within, found)
    return found


def unit_of(wide):
    wide = wide.astype(jnp.float32)
    length = jnp.sqrt(jnp.sum(wide * wide, axis=1, keepdims=True) + 1e-06)
    return wide / length, length


def weights_of(scal_ref, rows, columns, mine_ref, their_ref):
    s = lax.dot_general(mine_ref[...], their_ref[...], (((1,), (1,)), ((), ())), preferred_element_type=jnp.float32)
    label = jnp.where(rows == columns, 1.0, -1.0)
    d = 1.0 + jnp.exp(label * (scal_ref[0] * s + scal_ref[1]))
    r = pl.reciprocal(d, approx=True)
    r = r * (2.0 - d * r)
    return (-label * r).astype(jnp.bfloat16)


def pair_kernel(scal_ref, place_ref, me_ref, ml_ref, re_ref, rl_ref, *refs):
    *outs, their_ref = refs
    n = me_ref.shape[0]
    their_ref[:n, :] = re_ref[...]
    their_ref[n:, :] = rl_ref[...]
    mine_blocks, their_blocks = blocks_of(place_ref, True), blocks_of(place_ref, False)
    columns = column_ids(their_blocks, 0, 4)
    halves = [
        (k, weights_of(scal_ref, row_ids(mine_blocks, 2 * k, 2 * k + 2), columns, mine_ref, their_ref))
        for k, mine_ref in ((1, ml_ref), (0, me_ref))
    ]
    for k, w in halves:
        for start, width in ((0, 512), (512, 512), (1024, 128)):
            cols = pl.ds(start, width)
            g = jnp.dot(w, their_ref[:, cols], preferred_element_type=jnp.float32).astype(jnp.bfloat16)
            outs[2 * k][:, cols] = g[: n // 2]
            outs[2 * k + 1][:, cols] = g[n // 2 :]


def back_kernel(core_ref, scal_ref, img_ref, txt_ref, *refs):
    *mine, recv_ref, img_out, txt_out = refs

    def work(own_src, own_out, other_src, other_out):
        own = sum(ref[...].astype(jnp.float32) for ref in mine)
        for src, g, dst in ((own_src, own, own_out), (other_src, recv_ref[...].astype(jnp.float32), other_out)):
            unit, length = unit_of(src[...])
            g = scal_ref[0] * g[:ROWS]
            along = jnp.sum(unit * g, axis=1, keepdims=True)
            dst[...] = (g - unit * along) / length

    pl.when(core_ref[0] == 0)(lambda: work(img_ref, img_out, txt_ref, txt_out))
    pl.when(core_ref[0] == 1)(lambda: work(txt_ref, txt_out, img_ref, img_out))


def call(kernel, name, out_shape, scalars, args, flops=0, scratch=()):
    vmem = pl.BlockSpec(memory_space=pltpu.VMEM)
    return pl.pallas_call(
        kernel,
        out_shape=out_shape,
        scratch_shapes=list(scratch),
        in_specs=[pl.BlockSpec(memory_space=pltpu.SMEM)] * len(scalars) + [vmem] * len(args),
        out_specs=(vmem,) * len(out_shape),
        compiler_params=pltpu.CompilerParams(vmem_limit_bytes=VMEM),
        cost_estimate=pl.CostEstimate(flops=flops, bytes_accessed=1 << 20, transcendentals=0),
        name=name,
    )(*scalars, *args)


def on_device(images, texts, logarithmic_scale, similarity_bias):
    core = lax.axis_index("core")
    place = jnp.stack([lax.axis_index("x"), lax.axis_index("y"), lax.axis_index("zh") * 4 + lax.axis_index("zl"), core])
    scal = jnp.stack([jnp.exp(logarithmic_scale), similarity_bias])
    cores = core.reshape((1,))
    block = jax.ShapeDtypeStruct((PAD, D), jnp.bfloat16)
    both = jnp.stack([jnp.pad(v, ((0, PAD - ROWS), (0, 0))) for v in (images, texts)])
    keep, send = call(unit_kernel, "unit", (block, block), [cores], [both])
    held = jnp.concatenate([keep, core_swap(send)])
    for sources in ROUNDS[:-1]:
        held = jnp.concatenate([held] + [fetch(held, s) for s in sources])
    one, three, two = [fetch(held, s) for s in ROUNDS[-1]]
    me = jnp.concatenate([held, one])
    re = core_swap(me)
    scalars = [scal, place]
    n = me.shape[0]
    piece = jax.ShapeDtypeStruct((n // 2, D), jnp.bfloat16)
    flops = 4 * n * n * D

    ml = jnp.concatenate([three, two])
    rl = core_swap(ml)
    keep, p1, p3, p2 = call(
        pair_kernel, "pairs", (piece,) * 4, scalars, [me, ml, re, rl], 4 * flops, [pltpu.VMEM((2 * n, D), jnp.bfloat16)]
    )
    parts = [keep] + [fetch(p, s, True) for p, s in zip((p1, p3, p2), LAST)]
    for sources in reversed(BACK):
        n = parts[0].shape[0] // (len(sources) + 1)
        sends = [add([p[k * n : (k + 1) * n] for p in parts]) for k in range(1, len(sources) + 1)]
        parts = [p[:n] for p in parts] + [fetch(p, s, True) for p, s in zip(sends, sources)]
    recv = core_swap(add([p[PAD:] for p in parts]))
    wide = jax.ShapeDtypeStruct((ROWS, D), jnp.float32)
    return call(back_kernel, "back", (wide, wide), [cores, scal], [images, texts] + [p[:PAD] for p in parts] + [recv])


def solution(mesh):
    fine = Mesh(mesh.devices.reshape(SIZES), AXES)
    return jax.shard_map(
        on_device,
        mesh=fine,
        in_specs=(P(AXES, None), P(("zl", "y", "core", "zh", "x"), None), P(), P()),
        out_specs=(P(AXES, None), P(("zl", "y", "core", "zh", "x"), None)),
        check_vma=False,
    )
```
